256 devices in a mesh: side: 2 (over core), col: 32 (over z, y), hid: 4 (over x).
Axes of the slice: x: 4, y: 4, z: 8, core: 2. Of those that a mesh axis runs over, the one named last changes fastest.
Arguments:
- residual: bfloat16 [4096, 4096], P(('side', 'col', 'hid')), may hold values from -6 to 6
- queries: bfloat16 [4096, 4096], P(('side', 'col', 'hid')), may hold values from -37 to 37
- key_values: bfloat16 [4096, 256, 256], P(('side', 'col', 'hid')), may hold values from -13 to 13
- lengths: int32 [4096], P(('side', 'col', 'hid')), may hold values from 2 to 256, as said below
- route_ids: int32 [4096, 3], P(('side', 'col', 'hid')), may hold values from 0 to 31, all different within a row; in each aligned block of 16 rows (0 to 15, 16 to 31, ...) at most 2 rows name the same one
- route_weights: float32 [4096, 3], P(('side', 'col', 'hid')), may hold values from 0.1 to 1
- norm_gain: float32 [4096], replicated, may hold values from 0.1 to 1.9
- w_gate_up: bfloat16 [32, 4096, 2, 3072], P('col', None, None, ('side', 'hid')), may hold values from -0.09375 to 0.09375
- w_down: bfloat16 [32, 3072, 4096], P('col', ('side', 'hid')), may hold values from -0.109375 to 0.109375
Outputs:
- mixed: bfloat16 [4096, 4096], P(('side', 'col', 'hid'))
The draws below stay inside these ranges and needn't reach their ends.
Inputs may be any that keep to these rules, and one draw needn't show every extreme that they name: `lengths`: the live positions of a row are its first ones; some row has exactly 256. `route_ids`: a row names 3 different experts; among the rows of one device no expert is named more than 2 times, and one is named exactly 2 times.
All inputs are finite; a program needn't handle non-finite values.
Results may differ from the reference program's by a relative error of at most 0.0052.
Values may be sent and summed in bfloat16 or wider, within the bound.
A program may use at most 128 MiB of HBM per device.

```python
import math
import jax
import jax.numpy as jnp
import numpy as np
from jax import lax

D = 4096
HEADS = 32
HD = 128
FF = 3072
TOP = 3
RMB = 16
LMAX = 256
EXPERTS = 32
MOST = 2
ROWS = 4096


def draw_queries(key, part):
    key = jax.random.fold_in(key, 11)
    result = jnp.clip(jax.random.normal(key, (ROWS, HEADS, HD), jnp.float32), -4.0, 4.0)
    return result.reshape(ROWS, HEADS * HD).astype(jnp.bfloat16)


def draw_key_values(key, part):
    key = jax.random.fold_in(key, 12)
    result = jnp.clip(jax.random.normal(key, (ROWS, LMAX, 2 * HD), jnp.float32), -4.0, 4.0)
    return result.astype(jnp.bfloat16)


def draw_lengths(key, part):
    key = jax.random.fold_in(key, 13)
    first, second, third = jax.random.split(key, 3)
    devices_all = ROWS // RMB
    heavy = jax.random.randint(first, (devices_all,), 0, 4) == 0
    heavy = heavy.at[0].set(True)
    long_rows = jax.random.randint(second, (ROWS,), LMAX // 2, LMAX + 1)
    short_rows = jax.random.randint(third, (ROWS,), 2, LMAX // 4 + 1)
    result = jnp.where(jnp.repeat(heavy, RMB), long_rows, short_rows)
    return result.at[0].set(LMAX).astype(jnp.int32)


def steps_of(stream_key, extent, shards, low, top_value):
    gain = 1.0
    for position, blocks in shards:
        steps = jax.random.uniform(jax.random.fold_in(jax.random.fold_in(stream_key, 6), position), (blocks,), jnp.float32, low / len(shards), top_value / len(shards))
        gain = gain * jnp.repeat(jnp.exp(steps), extent[position] // blocks).reshape((-1,) + (1,) * (len(extent) - 1 - position))
    return gain


def assign_block(stream_key, own, number, rows, number_of, top, bound, lean):
    order = jax.random.permutation(stream_key, number_of)
    packed, ordinary = load_shares(number_of, rows * top, bound, lean, True), load_shares(number_of, rows * top, bound, lean, False)
    places = jnp.arange(number_of)

    def named(tallies, rotation):
        used = int((tallies > 0).sum())
        fixed = max(1, used // 4)
        moved = fixed + (places - fixed + rotation * (used - fixed)) % max(1, number_of - fixed)
        return jnp.zeros((number_of,), jnp.int32).at[order[jnp.where(places < fixed, places, moved)]].set(jnp.asarray(tallies, jnp.int32))

    tallies = jnp.where(number % 4 == 0, named(packed, number // 4), named(ordinary, number - number // 4 - 1))
    mixed = jax.random.permutation(jax.random.fold_in(own, 3), number_of)
    source_of, receiver = mixed[0:number_of // 2 * 2:2], mixed[1:number_of // 2 * 2:2]
    slack = jnp.minimum(tallies[source_of] - 1, bound - tallies[receiver]) // 2
    slack = jnp.where((source_of == order[0]) | (receiver == order[0]) | (tallies[receiver] == 0), 0, jnp.maximum(slack, 0))
    moved = jax.random.randint(jax.random.fold_in(own, 4), (number_of // 2,), 0, 1 << 20) % (slack + 1)
    tallies = tallies.at[source_of].add(-moved).at[receiver].add(moved)
    items = jnp.searchsorted(jnp.cumsum(tallies), jnp.arange(rows * top), side="right").astype(jnp.int32)
    table = items.reshape(top, rows).T
    table = table[jax.random.permutation(jax.random.fold_in(own, 1), rows)]
    rotation = jax.random.randint(jax.random.fold_in(own, 2), (rows, 1), 0, top)
    return jnp.take_along_axis(table, (jnp.arange(top)[None, :] + rotation) % top, axis=1)


def load_shares(count, total, reach, skew, full):
    weights = [(1 << 20) // math.isqrt(standing ** skew) + 1 for standing in range(1, count + 1)]
    largest = reach if full else min(reach, max(-(-total // count), total * weights[0] // sum(weights)))
    least = 1 if total - largest >= count - 1 else 0
    holding, surplus = [largest] + [least] * (count - 1), total - largest - least * (count - 1)
    while surplus > 0:
        candidates = [i for i in range(1, count) if holding[i] < largest] or [i for i in range(1, count) if holding[i] < reach]
        mass, remaining = sum([weights[i] for i in candidates]), surplus
        for i in candidates:
            extra = min(reach - holding[i], max(1, remaining * weights[i] // mass), surplus)
            holding[i] = holding[i] + extra
            surplus = surplus - extra
    return np.array(holding)


def bell_draw(own_key, shape, scale, reach, shards=(), kind=jnp.bfloat16):
    drawn = jax.random.normal(own_key, shape, jnp.float32) * scale
    if len(shards) > 0:
        drawn = steps_of(own_key, shape, shards, -0.22, 0.18) * drawn
    return jnp.clip(drawn, min=-reach, max=reach).astype(kind)


def setup_inputs(seed: int = 0) -> dict:
    key_list = jax.random.split(jax.random.key(seed), 10)
    residual = bell_draw(key_list[0], (ROWS, D), 1.0, 6.0, ((0, 256),))
    queries = draw_queries(jax.random.fold_in(key_list[9], 71), 0)
    key_values = draw_key_values(jax.random.fold_in(key_list[9], 71), 0)
    lengths = draw_lengths(jax.random.fold_in(key_list[9], 71), 0)
    route_ids_keys = jax.random.split(jax.random.fold_in(key_list[4], 1), ROWS // RMB)
    route_ids_turns = jax.random.permutation(jax.random.fold_in(key_list[4], 3), ROWS // RMB)
    route_ids = jax.vmap(lambda own, number: assign_block(jax.random.fold_in(key_list[4], 2), own, number, RMB, EXPERTS, TOP, MOST, 2))(route_ids_keys, route_ids_turns).reshape((ROWS, TOP))
    route_weights = jnp.clip(0.1 + 0.9 * jax.random.uniform(key_list[5], (ROWS, TOP), jnp.float32) ** steps_of(key_list[5], (ROWS, TOP), ((0, 256),), -0.2, 0.2), 0.1, 1.0)
    norm_gain = jnp.clip(1.0 + 0.18 * jax.random.normal(key_list[6], (D,), jnp.float32), 0.1, 1.9)
    w_gate_up = bell_draw(key_list[7], (EXPERTS, D, 2, FF), D ** -0.5, 0.09375, ((0, 32), (3, 8)))
    w_down = bell_draw(key_list[8], (EXPERTS, FF, D), FF ** -0.5, 0.109375, ((0, 32), (1, 8)))
    return dict(residual=residual, queries=queries, key_values=key_values, lengths=lengths, route_ids=route_ids, route_weights=route_weights, norm_gain=norm_gain, w_gate_up=w_gate_up, w_down=w_down)


def attend(parts):
    queries, key_values, lengths = parts
    row_count = queries.shape[0]
    heads_q = queries.reshape(row_count, HEADS, HD).astype(jnp.float32)
    key_rows = key_values[:, :, :HD].astype(jnp.float32)
    value_rows = key_values[:, :, HD:].astype(jnp.float32)
    scores = jnp.einsum('rhd,rtd->rht', heads_q, key_rows) * (1.0 / math.sqrt(HD))
    positions = jnp.arange(key_values.shape[1], dtype=jnp.int32)
    visible = positions[None, None, :] < lengths[:, None, None]
    scores = jnp.where(visible, scores, -1e+30)
    row_peak = lax.optimization_barrier(jnp.max(scores, axis=2, keepdims=True))
    exponent = jnp.where(visible, jnp.exp(scores - row_peak), 0.0)
    normalized = (exponent / lax.optimization_barrier(jnp.sum(exponent, axis=2, keepdims=True))).astype(jnp.bfloat16)
    heads_out = jnp.einsum('rht,rtd->rhd', normalized.astype(jnp.float32), value_rows)
    return heads_out.reshape(row_count, HEADS * HD)

def reference(residual, queries, key_values, lengths, route_ids, route_weights, norm_gain, w_gate_up, w_down):
    blocks = ROWS // RMB
    attended = lax.map(attend, (queries.reshape(blocks, RMB, D), key_values.reshape(blocks, RMB, LMAX, 2 * HD), lengths.reshape(blocks, RMB))).reshape(ROWS, D)
    hidden_state = residual.astype(jnp.float32) + attended
    mean_square = lax.optimization_barrier(jnp.mean(hidden_state * hidden_state, axis=1, keepdims=True))
    normed = (hidden_state * lax.rsqrt(mean_square + 1e-06) * norm_gain[None, :]).astype(jnp.bfloat16)
    capacity = MOST * blocks

    def one_expert(total, expert):
        chosen = route_ids == expert
        weight_row = lax.optimization_barrier(jnp.sum(jnp.where(chosen, route_weights, 0.0), axis=1))
        picked = jnp.any(chosen, axis=1)
        index_rows = jnp.nonzero(picked, size=capacity, fill_value=0)[0].astype(jnp.int32)
        live = jnp.arange(capacity, dtype=jnp.int32) < jnp.sum(picked.astype(jnp.int32))
        inputs = normed[index_rows]
        weights_gu = w_gate_up[expert]
        gate = jnp.dot(inputs, weights_gu[:, 0, :], preferred_element_type=jnp.float32)
        upper = jnp.dot(inputs, weights_gu[:, 1, :], preferred_element_type=jnp.float32)
        activ = (jax.nn.silu(gate) * upper).astype(jnp.bfloat16)
        output = jnp.dot(activ, w_down[expert], preferred_element_type=jnp.float32).astype(jnp.bfloat16)
        output = lax.optimization_barrier(output).astype(jnp.float32)
        contrib = jnp.where(live[:, None], weight_row[index_rows][:, None] * output, 0.0)
        return (total.at[index_rows].add(contrib), None)
    total, _ = lax.scan(one_expert, jnp.zeros((ROWS, D), jnp.float32), jnp.arange(EXPERTS, dtype=jnp.int32))
    return (hidden_state + total).astype(jnp.bfloat16)
```

```python
import math

import jax
import jax.numpy as jnp
from jax import lax
from jax.experimental import pallas as pl
from jax.experimental.pallas import tpu as pltpu
from jax.sharding import PartitionSpec as P

HEADS = 32
HD = 128
COLS = 32
NY = 4
NZ = 8
NX = 4
GROUPS = 4
PER = 8
CHUNK = 512
DZ = (0, 1, -2, 3, -3, 4, -1, 2)
MESH = pl.DeviceIdType.MESH
F32 = jnp.float32
BF16 = jnp.bfloat16


def iota(shape, axis):
    return lax.broadcasted_iota(jnp.int32, shape, axis)


def kernel(
    q_ref, res_ref, kv_ref, len_ref, ids_ref, rw_ref, gain_ref, wgu_hbm, wd_hbm,
    out_ref,
    qf, sc, att, hid, ns, tmp_i, tmp_w, sel, wt_hi, wt_lo, acc,
    disp, arr, rsend, ret, x, pf, pown, r1, sa, ta, sb, fin,
    wraw, wgu, wd,
    w_sem, d_send, d_recv, g_send, g_recv, r_send, r_recv, e_send, e_recv,
):
    side = lax.axis_index("side")
    col = lax.axis_index("col")
    hidx = lax.axis_index("hid")
    zc = col // NY
    yc = lax.rem(col, NY)
    rows, width = res_ref.shape
    half = width // 2

    def column(i, sign):
        dz, dy = DZ[i // NY], i % NY
        return lax.rem(zc + (sign * dz + NZ), NZ) * NY + lax.rem(yc + (sign * dy + NY), NY)

    def on_col(i, sign):
        return {"side": side, "col": column(i, sign), "hid": hidx}

    up = {"side": side, "col": col, "hid": lax.rem(hidx + 1, NX)}
    down = {"side": side, "col": col, "hid": lax.rem(hidx + NX - 1, NX)}
    partner = {"side": 1 - side, "col": col, "hid": hidx}

    def remote(src, dst, send, recv, device):
        return pltpu.make_async_remote_copy(
            src_ref=src, dst_ref=dst, send_sem=send, recv_sem=recv,
            device_id=device, device_id_type=MESH,
        )

    barrier = pltpu.get_barrier_semaphore()
    for device in [on_col(i, 1) for i in range(1, COLS)] + [up, down, partner]:
        pl.semaphore_signal(barrier, inc=1, device_id=device, device_id_type=MESH)

    w_copies = [
        pltpu.make_async_copy(
            wgu_hbm.at[:, :, pl.ds(l * 128, 128)],
            wraw.at[l],
            w_sem.at[l],
        )
        for l in range(3)
    ] + [pltpu.make_async_copy(wd_hbm, wd, w_sem.at[3])]
    for copy in w_copies:
        copy.start()

    tmp_i[...] = jnp.zeros_like(tmp_i)
    tmp_w[...] = jnp.zeros_like(tmp_w)
    tmp_i[0:3, 0:rows] = ids_ref[...]
    tmp_w[0:3, 0:rows] = rw_ref[...]
    ids_all = tmp_i[...]
    w_all = tmp_w[...]
    for shift in (16, 32, 64):
        ids_all = ids_all + pltpu.roll(ids_all, shift, 1)
        w_all = w_all + pltpu.roll(w_all, shift, 1)
    square = (128, 128)
    lane, sub = iota(square, 1), iota(square, 0)
    earlier = jnp.where(
        ((sub >> 4) == (lane >> 4)) & ((sub & 15) < (lane & 15)), 1.0, 0.0
    ).astype(BF16)
    same_part = (sub & 7) == (lane >> 4)
    rank_want = ((sub >> 3) & 1).astype(F32)
    for g in range(GROUPS):
        dz = jnp.where((sub >> 6) == 0, DZ[2 * g], DZ[2 * g + 1])
        dy = (sub >> 4) & 3
        expert = ((zc + dz + NZ) & (NZ - 1)) * NY + ((yc + dy) & (NY - 1))
        named = jnp.zeros(square, F32)
        weight = jnp.zeros(square, F32)
        for k in range(3):
            hit = expert == ids_all[k : k + 1, :]
            named = named + jnp.where(hit, 1.0, 0.0)
            weight = weight + jnp.where(hit, w_all[k : k + 1, :], 0.0)
        rank = jnp.dot(named.astype(BF16), earlier, preferred_element_type=F32)
        here = (named > 0.5) & (jnp.abs(rank - rank_want) < 0.5) & same_part
        sel[g] = jnp.where(here, 1.0, 0.0).astype(BF16)
        weight_t = jnp.where(here, weight, 0.0).T
        high = weight_t.astype(BF16)
        wt_hi[g] = high
        wt_lo[g] = (weight_t - high.astype(F32)).astype(BF16)

    for head in range(HEADS):
        qf[pl.ds(head * rows, rows), :] = q_ref[:, pl.ds(head * HD, HD)].astype(F32)
    positions = iota((HEADS, kv_ref.shape[1]), 1)
    for r in range(rows):
        q_r = qf[pl.ds(r, HEADS, stride=rows), :].astype(BF16)
        s_r = lax.dot_general(
            q_r, kv_ref[r, :, 0:HD], (((1,), (1,)), ((), ())), preferred_element_type=F32
        ) * (1.0 / math.sqrt(HD))
        sc[pl.ds(r * HEADS, HEADS), :] = jnp.where(positions < len_ref[r], s_r, -1e30)
    for r in range(rows):
        s_r = sc[pl.ds(r * HEADS, HEADS), :]
        e_r = jnp.exp(s_r - jnp.max(s_r, axis=1, keepdims=True))
        p_r = (e_r / jnp.sum(e_r, axis=1, keepdims=True)).astype(BF16)
        att[pl.ds(r, HEADS, stride=rows), :] = jnp.dot(
            p_r, kv_ref[r, :, HD : 2 * HD], preferred_element_type=F32
        )
    total = jnp.zeros((rows, HD), F32)
    for head in range(HEADS):
        lanes = pl.ds(head * HD, HD)
        h_part = res_ref[:, lanes].astype(F32) + att[pl.ds(head * rows, rows), :]
        hid[:, lanes] = h_part
        total = total + h_part * h_part
    scale = lax.rsqrt(jnp.sum(total, axis=1, keepdims=True) * (1.0 / width) + 1e-6)
    for j in range(PER):
        lanes = pl.ds(j * CHUNK, CHUNK)
        ns[pl.ds(j * rows, rows), :] = (hid[:, lanes] * scale * gain_ref[:, lanes]).astype(BF16)

    def d_copy(i):
        return remote(disp.at[i], arr.at[i], d_send.at[i], d_recv.at[i], on_col(i, 1))

    pl.semaphore_wait(barrier, COLS - 1 + 3)
    for g in range(GROUPS):
        block = jnp.dot(sel[g], ns[...], preferred_element_type=F32).astype(BF16)
        for k in range(PER):
            i = g * PER + k
            piece = block[k * 16 : (k + 1) * 16, :]
            if i == 0:
                arr[0] = piece
            else:
                disp[i] = piece
        for i in range(max(1, g * PER), (g + 1) * PER):
            d_copy(i).start()

    to_rows = jnp.where(
        lane == ((sub & 15) >> 1) * 16 + (sub & 1) * 8 + (sub >> 4), 1.0, 0.0
    ).astype(BF16)
    to_blocks = jnp.where(
        lane == (sub & 7) * 16 + (sub >> 4) * 2 + ((sub >> 3) & 1), 1.0, 0.0
    ).astype(BF16)

    wide = (256, 256)
    apart = jnp.where(
        iota(wide, 1) == 2 * (iota(wide, 0) & 127) + (iota(wide, 0) >> 7), 1.0, 0.0
    ).astype(BF16)

    def take_apart(l):
        w_copies[l].wait()
        raw = wraw.at[l].reshape(8192, 128)

        def body(t, carry):
            start = pl.multiple_of(t * 256, 256)
            pair = jnp.dot(
                apart, raw[pl.ds(start, 256), :], preferred_element_type=F32
            ).astype(BF16)
            there = pl.ds(pl.multiple_of(t * 128, 128), 128)
            wgu[l, there, 0:128] = pair[0:128, :]
            wgu[l, there, 128:256] = pair[128:256, :]
            return carry

        lax.fori_loop(0, 32, body, 0, unroll=4)

    def g_copy(g, which):
        src, dst, device = {
            0: (x.at[g, 0, 0], x.at[g, 0, 1], up),
            1: (x.at[g, 0, 0], x.at[g, 0, 2], down),
            2: (x.at[g, 0, 1, :, pl.ds(0, half)], x.at[g, 0, 3, :, pl.ds(0, half)], up),
            3: (x.at[g, 0, 2, :, pl.ds(half, half)], x.at[g, 0, 3, :, pl.ds(half, half)], down),
            4: (x.at[g, 0, 0], x.at[g, 1, 0], partner),
            5: (x.at[g, 0, 1], x.at[g, 1, 1], partner),
            6: (x.at[g, 0, 2], x.at[g, 1, 2], partner),
            7: (x.at[g, 0, 3], x.at[g, 1, 3], partner),
        }[which]
        return remote(src, dst, g_send.at[g, which], g_recv.at[g, which], device)

    def gather_own(g):
        for i in range(max(1, g * PER), (g + 1) * PER):
            d_copy(i).wait_recv()
        blocks = arr[pl.ds(g * PER, PER)].reshape(128, CHUNK)
        rows_g = jnp.dot(to_rows, blocks, preferred_element_type=F32).astype(BF16)
        for j in range(PER):
            x[g, 0, 0, :, pl.ds(j * CHUNK, CHUNK)] = rows_g[j * 16 : (j + 1) * 16, :]
        for which in (0, 1, 4):
            g_copy(g, which).start()

    def gather_on(g):
        g_copy(g, 0).wait_recv()
        g_copy(g, 2).start()
        g_copy(g, 5).start()
        g_copy(g, 1).wait_recv()
        g_copy(g, 3).start()
        g_copy(g, 6).start()

    def gather_far(g):
        g_copy(g, 2).wait_recv()
        g_copy(g, 3).wait_recv()
        g_copy(g, 7).start()

    def r_copy(g, which):
        low, high = pl.ds(0, half), pl.ds(half, half)
        src, dst, device = {
            0: (pown.at[g], r1.at[g], partner),
            1: (sa.at[g, 0], ta.at[g, 0], up),
            2: (sa.at[g, 1], ta.at[g, 1], down),
            3: (sa.at[g, 2], fin.at[g, 0, :, high], up),
            4: (sa.at[g, 3], fin.at[g, 1, :, low], down),
            5: (sb.at[g, 0], fin.at[g, 0, :, low], up),
            6: (sb.at[g, 1], fin.at[g, 1, :, high], down),
        }[which]
        return remote(src, dst, r_send.at[g, which], r_recv.at[g, which], device)

    def experts(g):
        for which in (4, 5, 6, 7):
            g_copy(g, which).wait_recv()
        rows_g = x[g].reshape(128, width)
        parts = []
        for l in range(3):
            both = jnp.dot(rows_g, wgu[l], preferred_element_type=F32)
            gate, upper = both[:, 0:128], both[:, 128:256]
            parts.append((gate / (1.0 + jnp.exp(-gate)) * upper).astype(BF16))
        act = jnp.concatenate(parts, axis=1)
        for n in range(8):
            lanes = pl.ds(n * CHUNK, CHUNK)
            part = jnp.dot(act, wd[:, lanes], preferred_element_type=F32)
            pf[g, :, lanes] = part[0:64, :]
            for rel in range(4):
                pown[g, rel, :, lanes] = part[64 + rel * 16 : 80 + rel * 16, :].astype(BF16)
        r_copy(g, 0).start()

    def chip_sum(g):
        r_copy(g, 0).wait_recv()
        low, high = pl.ds(0, half), pl.ds(half, half)

        def both(rel, lanes):
            return pf[g, pl.ds(rel * 16, 16), lanes] + r1[g, rel, :, lanes].astype(F32)

        sa[g, 0] = both(3, low).astype(BF16)
        r_copy(g, 1).start()
        sa[g, 1] = both(3, high).astype(BF16)
        r_copy(g, 2).start()
        sa[g, 2] = both(2, high).astype(BF16)
        r_copy(g, 3).start()
        sa[g, 3] = both(1, low).astype(BF16)
        r_copy(g, 4).start()

    def pass_on(g):
        low, high = pl.ds(0, half), pl.ds(half, half)

        def both(rel, lanes):
            return pf[g, pl.ds(rel * 16, 16), lanes] + r1[g, rel, :, lanes].astype(F32)

        r_copy(g, 1).wait_recv()
        sb[g, 0] = (both(2, low) + ta[g, 0].astype(F32)).astype(BF16)
        r_copy(g, 5).start()
        r_copy(g, 2).wait_recv()
        sb[g, 1] = (both(1, high) + ta[g, 1].astype(F32)).astype(BF16)
        r_copy(g, 6).start()

    def e_copy(i):
        return remote(rsend.at[i], ret.at[i], e_send.at[i], e_recv.at[i], on_col(i, -1))

    def give_back(g):
        for which in (3, 4, 5, 6):
            r_copy(g, which).wait_recv()
        pieces = []
        for j in range(PER):
            lanes = pl.ds(j * CHUNK, CHUNK)
            whole = pf[g, 0:16, lanes] + r1[g, 0, :, lanes].astype(F32)
            whole = whole + fin[g, 0, :, lanes].astype(F32) + fin[g, 1, :, lanes].astype(F32)
            pieces.append(whole.astype(BF16))
        blocks = jnp.dot(
            to_blocks, jnp.concatenate(pieces, axis=0), preferred_element_type=F32
        ).astype(BF16)
        for k in range(PER):
            i = g * PER + k
            piece = blocks[k * 16 : (k + 1) * 16, :]
            if i == 0:
                ret[0] = piece
            else:
                rsend[i] = piece
        for i in range(max(1, g * PER), (g + 1) * PER):
            e_copy(i).start()

    def combine(g):
        for i in range(max(1, g * PER), (g + 1) * PER):
            e_copy(i).wait_recv()
        blocks = ret[pl.ds(g * PER, PER)].reshape(128, CHUNK)
        part = jnp.dot(wt_hi[g], blocks, preferred_element_type=F32) + jnp.dot(
            wt_lo[g], blocks, preferred_element_type=F32
        )
        if g == 0:
            acc[...] = part
        else:
            acc[...] = acc[...] + part

    take_apart(0)
    gather_own(0)
    take_apart(1)
    gather_own(1)
    take_apart(2)
    gather_on(0)
    gather_far(0)
    gather_on(1)
    gather_own(2)
    w_copies[3].wait()
    experts(0)
    gather_far(1)
    chip_sum(0)
    gather_on(2)
    gather_own(3)
    experts(1)
    pass_on(0)
    gather_far(2)
    chip_sum(1)
    gather_on(3)
    experts(2)
    give_back(0)
    pass_on(1)
    gather_far(3)
    chip_sum(2)
    experts(3)
    give_back(1)
    pass_on(2)
    chip_sum(3)
    combine(0)
    give_back(2)
    pass_on(3)
    combine(1)
    give_back(3)
    combine(2)
    combine(3)

    for j in range(PER):
        lanes = pl.ds(j * CHUNK, CHUNK)
        out_ref[:, lanes] = (hid[:, lanes] + acc[pl.ds(j * rows, rows), :]).astype(BF16)

    for i in range(1, COLS):
        d_copy(i).wait_send()
        e_copy(i).wait_send()
    for g in range(GROUPS):
        for which in range(8):
            g_copy(g, which).wait_send()
        for which in range(7):
            r_copy(g, which).wait_send()


def on_device(
    residual, queries, key_values, lengths, route_ids, route_weights, norm_gain, w_gate_up, w_down
):
    rows, width = residual.shape
    vmem = pl.BlockSpec(memory_space=pltpu.VMEM)
    anywhere = pl.BlockSpec(memory_space=pl.ANY)
    half = width // 2
    return pl.pallas_call(
        kernel,
        out_shape=jax.ShapeDtypeStruct((rows, width), BF16),
        in_specs=[
            vmem, vmem, vmem, pl.BlockSpec(memory_space=pltpu.SMEM), vmem, vmem, vmem,
            anywhere, anywhere,
        ],
        out_specs=vmem,
        scratch_shapes=[
            pltpu.VMEM((HEADS * rows, HD), F32),
            pltpu.VMEM((HEADS * rows, key_values.shape[1]), F32),
            pltpu.VMEM((HEADS * rows, HD), F32),
            pltpu.VMEM((rows, width), F32),
            pltpu.VMEM((PER * rows, CHUNK), BF16),
            pltpu.VMEM((8, 128), jnp.int32),
            pltpu.VMEM((8, 128), F32),
            pltpu.VMEM((GROUPS, 128, 128), BF16),
            pltpu.VMEM((GROUPS, 128, 128), BF16),
            pltpu.VMEM((GROUPS, 128, 128), BF16),
            pltpu.VMEM((PER * rows, CHUNK), F32),
            pltpu.VMEM((COLS, 16, CHUNK), BF16),
            pltpu.VMEM((COLS, 16, CHUNK), BF16),
            pltpu.VMEM((COLS, 16, CHUNK), BF16),
            pltpu.VMEM((COLS, 16, CHUNK), BF16),
            pltpu.VMEM((GROUPS, 2, 4, 16, width), BF16),
            pltpu.VMEM((GROUPS, 64, width), F32),
            pltpu.VMEM((GROUPS, 4, 16, width), BF16),
            pltpu.VMEM((GROUPS, 4, 16, width), BF16),
            pltpu.VMEM((GROUPS, 4, 16, half), BF16),
            pltpu.VMEM((GROUPS, 2, 16, half), BF16),
            pltpu.VMEM((GROUPS, 2, 16, half), BF16),
            pltpu.VMEM((GROUPS, 2, 16, width), BF16),
            pltpu.VMEM((3, 4096, 2, 128), BF16),
            pltpu.VMEM((3, 4096, 256), BF16),
            pltpu.VMEM((384, 4096), BF16),
            pltpu.SemaphoreType.DMA((4,)),
            pltpu.SemaphoreType.DMA((COLS,)),
            pltpu.SemaphoreType.DMA((COLS,)),
            pltpu.SemaphoreType.DMA((GROUPS, 8)),
            pltpu.SemaphoreType.DMA((GROUPS, 8)),
            pltpu.SemaphoreType.DMA((GROUPS, 7)),
            pltpu.SemaphoreType.DMA((GROUPS, 7)),
            pltpu.SemaphoreType.DMA((COLS,)),
            pltpu.SemaphoreType.DMA((COLS,)),
        ],
        compiler_params=pltpu.CompilerParams(
            collective_id=0, has_side_effects=True, vmem_limit_bytes=60 * 2**20
        ),
        name="moe_step",
    )(
        queries, residual, key_values, lengths, route_ids.T, route_weights.T,
        norm_gain.reshape(1, width), w_gate_up[0], w_down[0],
    )


def solution(mesh):
    placed = (
        P(("side", "col", "hid"), None),
        P(("side", "col", "hid"), None),
        P(("side", "col", "hid"), None, None),
        P(("side", "col", "hid")),
        P(("side", "col", "hid"), None),
        P(("side", "col", "hid"), None),
        P(),
        P("col", None, None, ("side", "hid")),
        P("col", ("side", "hid"), None),
    )
    return jax.shard_map(
        on_device,
        mesh=mesh,
        in_specs=placed,
        out_specs=P(("side", "col", "hid"), None),
        check_vma=False,
    )
```

```python
import math

import jax
import jax.numpy as jnp
from jax import lax
from jax.experimental import pallas as pl
from jax.experimental.pallas import tpu as pltpu
from jax.sharding import PartitionSpec as P

HEADS = 32
HD = 128
COLS = 32
NY = 4
NZ = 8
NX = 4
GROUPS = 4
PER = 8
CHUNK = 512
DZ = (0, 1, -2, 3, -3, 4, -1, 2)
SCHEDULE = (
    ("apart", 0), ("apart", 1), ("apart", 2), ("apart", 3), ("own", 0),
    ("down", 0), ("up", 0), ("own", 1), ("own", 2), ("up", 1),
    ("down", 1), ("own", 3), ("up", 2), ("down", 2), ("experts", 1),
    ("down", 3), ("up", 3), ("experts", 2), ("pass_down", 1), ("pass_up", 1),
    ("experts", 0), ("pass_up", 2), ("pass_down", 2), ("back", 1), ("experts", 3),
    ("back", 2), ("pass_up", 0), ("pass_down", 0), ("pass_up", 3), ("pass_down", 3),
    ("back", 0), ("back", 3), ("combine", 0), ("combine", 1), ("combine", 2),
    ("combine", 3),
)
MESH = pl.DeviceIdType.MESH
F32 = jnp.float32
BF16 = jnp.bfloat16


def iota(shape, axis):
    return lax.broadcasted_iota(jnp.int32, shape, axis)


def kernel(
    q_ref, res_ref, kv_ref, len_ref, ids_ref, rw_ref, gain_ref, wgu_hbm, wd_hbm,
    out_ref,
    qf, sc, att, hid, ns, tmp_i, tmp_w, sel, wt_hi, wt_lo, acc,
    disp, arr, rsend, ret, x, pf, sa, ta, sb, fin,
    wraw, wgu, wd,
    w_sem, p_send, p_recv, d_send, d_recv, g_send, g_recv, r_send, r_recv, e_send, e_recv,
):
    side = lax.axis_index("side")
    col = lax.axis_index("col")
    hidx = lax.axis_index("hid")
    zc = col // NY
    yc = lax.rem(col, NY)
    rows, width = res_ref.shape
    half = width // 2

    def column(i, sign):
        dz, dy = DZ[i // NY], i % NY
        return lax.rem(zc + (sign * dz + NZ), NZ) * NY + lax.rem(yc + (sign * dy + NY), NY)

    def on_col(i, sign):
        return {"side": side, "col": column(i, sign), "hid": hidx}

    up = {"side": side, "col": col, "hid": lax.rem(hidx + 1, NX)}
    down = {"side": side, "col": col, "hid": lax.rem(hidx + NX - 1, NX)}
    partner = {"side": 1 - side, "col": col, "hid": hidx}

    def remote(src, dst, send, recv, device):
        return pltpu.make_async_remote_copy(
            src_ref=src, dst_ref=dst, send_sem=send, recv_sem=recv,
            device_id=device, device_id_type=MESH,
        )

    begun, landed = [], set()

    def start(make, *key):
        make(*key).start()
        begun.append((make, key))

    def arrive(make, *key):
        make(*key).wait_recv()
        landed.add((make, key))

    barrier = pltpu.get_barrier_semaphore()
    for device in [on_col(i, 1) for i in range(1, COLS)] + [up, down, partner]:
        pl.semaphore_signal(barrier, inc=1, device_id=device, device_id_type=MESH)

    w_copies = [
        pltpu.make_async_copy(
            wgu_hbm.at[:, :, pl.ds(l * 128, 128)],
            wraw.at[l],
            w_sem.at[l],
        )
        for l in range(3)
    ] + [pltpu.make_async_copy(wd_hbm, wd.at[pl.ds(0, 384)], w_sem.at[3])]
    for copy in w_copies:
        copy.start()

    tmp_i[...] = jnp.zeros_like(tmp_i)
    tmp_w[...] = jnp.zeros_like(tmp_w)
    tmp_i[0:3, 0:rows] = ids_ref[...]
    tmp_w[0:3, 0:rows] = rw_ref[...]
    ids_all = tmp_i[...]
    w_all = tmp_w[...]
    for shift in (16, 32, 64):
        ids_all = ids_all + pltpu.roll(ids_all, shift, 1)
        w_all = w_all + pltpu.roll(w_all, shift, 1)
    square = (128, 128)
    lane, sub = iota(square, 1), iota(square, 0)
    earlier = jnp.where(
        ((sub >> 4) == (lane >> 4)) & ((sub & 15) < (lane & 15)), 1.0, 0.0
    ).astype(BF16)
    same_part = (sub & 7) == (lane >> 4)
    rank_want = ((sub >> 3) & 1).astype(F32)
    for g in range(GROUPS):
        dz = jnp.where((sub >> 6) == 0, DZ[2 * g], DZ[2 * g + 1])
        dy = (sub >> 4) & 3
        expert = ((zc + dz + NZ) & (NZ - 1)) * NY + ((yc + dy) & (NY - 1))
        named = jnp.zeros(square, F32)
        weight = jnp.zeros(square, F32)
        for k in range(3):
            hit = expert == ids_all[k : k + 1, :]
            named = named + jnp.where(hit, 1.0, 0.0)
            weight = weight + jnp.where(hit, w_all[k : k + 1, :], 0.0)
        rank = jnp.dot(named.astype(BF16), earlier, preferred_element_type=F32)
        here = (named > 0.5) & (jnp.abs(rank - rank_want) < 0.5) & same_part
        sel[g] = jnp.where(here, 1.0, 0.0).astype(BF16)
        weight_t = jnp.where(here, weight, 0.0).T
        high = weight_t.astype(BF16)
        wt_hi[g] = high
        wt_lo[g] = (weight_t - high.astype(F32)).astype(BF16)

    for head in range(HEADS):
        qf[pl.ds(head * rows, rows), :] = q_ref[:, pl.ds(head * HD, HD)].astype(F32)
    positions = iota((HEADS, kv_ref.shape[1]), 1)
    for r in range(rows):
        q_r = qf[pl.ds(r, HEADS, stride=rows), :].astype(BF16)
        s_r = lax.dot_general(
            q_r, kv_ref[r, :, 0:HD], (((1,), (1,)), ((), ())), preferred_element_type=F32
        ) * (1.0 / math.sqrt(HD))
        sc[pl.ds(r * HEADS, HEADS), :] = jnp.where(positions < len_ref[r], s_r, -1e30)
    for r in range(rows):
        s_r = sc[pl.ds(r * HEADS, HEADS), :]
        e_r = jnp.exp(s_r - jnp.max(s_r, axis=1, keepdims=True))
        p_r = (e_r / jnp.sum(e_r, axis=1, keepdims=True)).astype(BF16)
        att[pl.ds(r, HEADS, stride=rows), :] = jnp.dot(
            p_r, kv_ref[r, :, HD : 2 * HD], preferred_element_type=F32
        )
    total = jnp.zeros((rows, HD), F32)
    for head in range(HEADS):
        lanes = pl.ds(head * HD, HD)
        h_part = res_ref[:, lanes].astype(F32) + att[pl.ds(head * rows, rows), :]
        hid[:, lanes] = h_part
        total = total + h_part * h_part
    scale = lax.rsqrt(jnp.sum(total, axis=1, keepdims=True) * (1.0 / width) + 1e-6)
    for j in range(PER):
        lanes = pl.ds(j * CHUNK, CHUNK)
        ns[pl.ds(j * rows, rows), :] = (hid[:, lanes] * scale * gain_ref[:, lanes]).astype(BF16)

    def d_copy(i):
        return remote(disp.at[i], arr.at[i], d_send.at[i], d_recv.at[i], on_col(i, 1))

    pl.semaphore_wait(barrier, COLS - 1 + 3)
    for g in range(GROUPS):
        block = jnp.dot(sel[g], ns[...], preferred_element_type=F32).astype(BF16)
        for k in range(PER):
            i = g * PER + k
            piece = block[k * 16 : (k + 1) * 16, :]
            if i == 0:
                arr[0] = piece
            else:
                disp[i] = piece
        for i in range(max(1, g * PER), (g + 1) * PER):
            start(d_copy, i)

    to_rows = jnp.where(
        lane == ((sub & 15) >> 1) * 16 + (sub & 1) * 8 + (sub >> 4), 1.0, 0.0
    ).astype(BF16)
    to_blocks = jnp.where(
        lane == (sub & 7) * 16 + (sub >> 4) * 2 + ((sub >> 3) & 1), 1.0, 0.0
    ).astype(BF16)

    wide = (256, 256)
    apart = jnp.where(
        iota(wide, 1) == 2 * (iota(wide, 0) & 127) + (iota(wide, 0) >> 7), 1.0, 0.0
    ).astype(BF16)

    def p_copy(which):
        if which == 4:
            src, dst = wd.at[pl.ds(0, 384)], wd.at[pl.ds(384, 384)]
        else:
            deep = pl.ds(which * 1024, 1024)
            src, dst = wgu.at[0, :, deep, :], wgu.at[1, :, deep, :]
        return remote(src, dst, p_send.at[which], p_recv.at[which], partner)

    def take_apart(part):
        if part == 0:
            w_copies[3].wait()
            start(p_copy, 4)
            for l in range(3):
                w_copies[l].wait()
        raws = [wraw.at[l].reshape(8192, 128) for l in range(3)]

        def body(t, carry):
            first = part * 2048 + t * 512
            both = jnp.concatenate(
                [raw[pl.ds(pl.multiple_of(first + d, 256), 256), :] for d in (0, 256) for raw in raws],
                axis=1,
            )
            pair = jnp.dot(apart, both, preferred_element_type=F32).astype(BF16)
            for d in range(2):
                there = pl.ds(pl.multiple_of(part * 1024 + t * 256 + d * 128, 128), 128)
                for l in range(3):
                    lanes = slice((d * 3 + l) * 128, (d * 3 + l + 1) * 128)
                    wgu[0, l, there, 0:128] = pair[0:128, lanes]
                    wgu[0, l, there, 128:256] = pair[128:256, lanes]
            return carry

        lax.fori_loop(0, 4, body, 0, unroll=2)
        start(p_copy, part)

    low, high = pl.ds(0, half), pl.ds(half, half)

    def g_copy(g, which):
        src, dst, device = {
            0: (x.at[g, 0, :, low], x.at[g, 1, :, low], up),
            1: (x.at[g, 0, :, high], x.at[g, 1, :, high], up),
            2: (x.at[g, 0, :, high], x.at[g, 2, :, high], down),
            3: (x.at[g, 0, :, low], x.at[g, 2, :, low], down),
            4: (x.at[g, 1, :, low], x.at[g, 3, :, low], up),
            5: (x.at[g, 2, :, high], x.at[g, 3, :, high], down),
        }[which]
        return remote(src, dst, g_send.at[g, which], g_recv.at[g, which], device)

    def gather_own(g):
        for i in range(max(1, g * PER), (g + 1) * PER):
            arrive(d_copy, i)
        blocks = arr[pl.ds(g * PER, PER)].reshape(128, CHUNK)
        rows_g = jnp.dot(to_rows, blocks, preferred_element_type=F32).astype(BF16)
        for j in range(PER):
            x[g, 0, :, pl.ds(j * CHUNK, CHUNK)] = rows_g[j * 16 : (j + 1) * 16, :]
        for which in (0, 2, 1, 3):
            start(g_copy, g, which)

    def on_up(g):
        arrive(g_copy, g, 0)
        start(g_copy, g, 4)

    def on_down(g):
        arrive(g_copy, g, 2)
        start(g_copy, g, 5)

    def r_copy(g, which):
        src, dst, device = {
            0: (sa.at[g, 0], ta.at[g, 0], up),
            1: (sa.at[g, 1], ta.at[g, 1], down),
            2: (sa.at[g, 2], fin.at[g, 0, :, high], up),
            3: (sa.at[g, 3], fin.at[g, 1, :, low], down),
            4: (sb.at[g, 0], fin.at[g, 0, :, low], up),
            5: (sb.at[g, 1], fin.at[g, 1, :, high], down),
        }[which]
        return remote(src, dst, r_send.at[g, which], r_recv.at[g, which], device)

    def experts(g):
        if not ready:
            for which in range(5):
                arrive(p_copy, which)
            ready.append(True)
        for which in (1, 3, 4, 5):
            arrive(g_copy, g, which)
        rows_g = x[g].reshape(64, width)
        parts = []
        for core in range(2):
            for l in range(3):
                both = jnp.dot(rows_g, wgu[core, l], preferred_element_type=F32)
                gate, upper = both[:, 0:128], both[:, 128:256]
                parts.append((gate / (1.0 + jnp.exp(-gate)) * upper).astype(BF16))
        act = jnp.concatenate(parts, axis=1)
        for n in range(8):
            lanes = pl.ds(n * CHUNK, CHUNK)
            there = pl.ds(n % 4 * CHUNK, CHUNK)
            part = jnp.dot(act, wd[:, lanes], preferred_element_type=F32)
            pf[g, 0:16, lanes] = part[0:16, :]
            if n < 4:
                sa[g, 0, :, there] = part[48:64, :].astype(BF16)
                sa[g, 3, :, there] = part[16:32, :].astype(BF16)
                pf[g, 32:48, lanes] = part[32:48, :]
            else:
                sa[g, 1, :, there] = part[48:64, :].astype(BF16)
                sa[g, 2, :, there] = part[32:48, :].astype(BF16)
                pf[g, 16:32, lanes] = part[16:32, :]
            if n == 3:
                start(r_copy, g, 0)
                start(r_copy, g, 3)
        start(r_copy, g, 1)
        start(r_copy, g, 2)

    def pass_up(g):
        arrive(r_copy, g, 0)
        sb[g, 0] = (pf[g, 32:48, low] + ta[g, 0].astype(F32)).astype(BF16)
        start(r_copy, g, 4)

    def pass_down(g):
        arrive(r_copy, g, 1)
        sb[g, 1] = (pf[g, 16:32, high] + ta[g, 1].astype(F32)).astype(BF16)
        start(r_copy, g, 5)

    def e_copy(i):
        return remote(rsend.at[i], ret.at[i], e_send.at[i], e_recv.at[i], on_col(i, -1))

    def give_back(g):
        for which in (2, 3, 4, 5):
            arrive(r_copy, g, which)
        pieces = []
        for j in range(PER):
            lanes = pl.ds(j * CHUNK, CHUNK)
            whole = pf[g, 0:16, lanes] + fin[g, 0, :, lanes].astype(F32) + fin[g, 1, :, lanes].astype(F32)
            pieces.append(whole.astype(BF16))
        blocks = jnp.dot(
            to_blocks, jnp.concatenate(pieces, axis=0), preferred_element_type=F32
        ).astype(BF16)
        for k in range(PER):
            i = g * PER + k
            piece = blocks[k * 16 : (k + 1) * 16, :]
            if i == 0:
                ret[0] = piece
            else:
                rsend[i] = piece
        for i in range(max(1, g * PER), (g + 1) * PER):
            start(e_copy, i)

    def combine(g):
        for i in range(max(1, g * PER), (g + 1) * PER):
            arrive(e_copy, i)
        blocks = ret[pl.ds(g * PER, PER)].reshape(128, CHUNK)
        part = jnp.dot(wt_hi[g], blocks, preferred_element_type=F32) + jnp.dot(
            wt_lo[g], blocks, preferred_element_type=F32
        )
        if not summed:
            summed.append(True)
            acc[...] = part
        else:
            acc[...] = acc[...] + part

    steps = {
        "apart": take_apart, "own": gather_own, "up": on_up, "down": on_down,
        "experts": experts, "pass_up": pass_up, "pass_down": pass_down, "back": give_back,
        "combine": combine,
    }
    ready, summed = [], []
    for name, number in SCHEDULE:
        steps[name](number)

    for j in range(PER):
        lanes = pl.ds(j * CHUNK, CHUNK)
        out_ref[:, lanes] = (hid[:, lanes] + acc[pl.ds(j * rows, rows), :]).astype(BF16)

    for make, key in begun:
        make(*key).wait_send()


def on_device(
    residual, queries, key_values, lengths, route_ids, route_weights, norm_gain, w_gate_up, w_down
):
    rows, width = residual.shape
    vmem = pl.BlockSpec(memory_space=pltpu.VMEM)
    anywhere = pl.BlockSpec(memory_space=pl.ANY)
    half = width // 2
    return pl.pallas_call(
        kernel,
        out_shape=jax.ShapeDtypeStruct((rows, width), BF16),
        in_specs=[
            vmem, vmem, vmem, pl.BlockSpec(memory_space=pltpu.SMEM), vmem, vmem, vmem,
            anywhere, anywhere,
        ],
        out_specs=vmem,
        scratch_shapes=[
            pltpu.VMEM((HEADS * rows, HD), F32),
            pltpu.VMEM((HEADS * rows, key_values.shape[1]), F32),
            pltpu.VMEM((HEADS * rows, HD), F32),
            pltpu.VMEM((rows, width), F32),
            pltpu.VMEM((PER * rows, CHUNK), BF16),
            pltpu.VMEM((8, 128), jnp.int32),
            pltpu.VMEM((8, 128), F32),
            pltpu.VMEM((GROUPS, 128, 128), BF16),
            pltpu.VMEM((GROUPS, 128, 128), BF16),
            pltpu.VMEM((GROUPS, 128, 128), BF16),
            pltpu.VMEM((PER * rows, CHUNK), F32),
            pltpu.VMEM((COLS, 16, CHUNK), BF16),
            pltpu.VMEM((COLS, 16, CHUNK), BF16),
            pltpu.VMEM((COLS, 16, CHUNK), BF16),
            pltpu.VMEM((COLS, 16, CHUNK), BF16),
            pltpu.VMEM((GROUPS, 4, 16, width), BF16),
            pltpu.VMEM((GROUPS, 48, width), F32),
            pltpu.VMEM((GROUPS, 4, 16, half), BF16),
            pltpu.VMEM((GROUPS, 2, 16, half), BF16),
            pltpu.VMEM((GROUPS, 2, 16, half), BF16),
            pltpu.VMEM((GROUPS, 2, 16, width), BF16),
            pltpu.VMEM((3, 4096, 2, 128), BF16),
            pltpu.VMEM((2, 3, 4096, 256), BF16),
            pltpu.VMEM((768, 4096), BF16),
            pltpu.SemaphoreType.DMA((4,)),
            pltpu.SemaphoreType.DMA((5,)),
            pltpu.SemaphoreType.DMA((5,)),
            pltpu.SemaphoreType.DMA((COLS,)),
            pltpu.SemaphoreType.DMA((COLS,)),
            pltpu.SemaphoreType.DMA((GROUPS, 6)),
            pltpu.SemaphoreType.DMA((GROUPS, 6)),
            pltpu.SemaphoreType.DMA((GROUPS, 6)),
            pltpu.SemaphoreType.DMA((GROUPS, 6)),
            pltpu.SemaphoreType.DMA((COLS,)),
            pltpu.SemaphoreType.DMA((COLS,)),
        ],
        compiler_params=pltpu.CompilerParams(
            collective_id=0, has_side_effects=True, vmem_limit_bytes=60 * 2**20
        ),
        name="moe_step",
    )(
        queries, residual, key_values, lengths, route_ids.T, route_weights.T,
        norm_gain.reshape(1, width), w_gate_up[0], w_down[0],
    )


def solution(mesh):
    placed = (
        P(("side", "col", "hid"), None),
        P(("side", "col", "hid"), None),
        P(("side", "col", "hid"), None, None),
        P(("side", "col", "hid")),
        P(("side", "col", "hid"), None),
        P(("side", "col", "hid"), None),
        P(),
        P("col", None, None, ("side", "hid")),
        P("col", ("side", "hid"), None),
    )
    return jax.shard_map(
        on_device,
        mesh=mesh,
        in_specs=placed,
        out_specs=P(("side", "col", "hid"), None),
        check_vma=False,
    )
```

```python
import math

import jax
import jax.numpy as jnp
from jax import lax
from jax.experimental import pallas as pl
from jax.experimental.pallas import tpu as pltpu
from jax.sharding import PartitionSpec as P

HEADS = 32
HD = 128
COLS = 32
NY = 4
NZ = 8
NX = 4
GROUPS = 4
PER = 8
CHUNK = 512
DZ = (0, 1, -2, 3, -3, 4, -1, 2)
SCHEDULE = (
    ("apart", 0), ("send", 2), ("apart", 1), ("send", 3), ("own", 0),
    ("apart", 2), ("apart", 3), ("down", 0), ("up", 0), ("weigh", 0),
    ("weigh", 1), ("weigh", 2), ("weigh", 3), ("own", 1), ("own", 2),
    ("up", 1), ("down", 1), ("own", 3), ("up", 2), ("down", 2),
    ("experts", 1), ("down", 3), ("up", 3), ("experts", 2), ("pass_down", 1),
    ("pass_up", 1), ("experts", 0), ("pass_up", 2), ("pass_down", 2), ("back", 1),
    ("experts", 3), ("back", 2), ("pass_up", 0), ("pass_down", 0), ("pass_up", 3),
    ("pass_down", 3), ("back", 0), ("back", 3), ("combine", 0), ("combine", 1),
    ("combine", 2), ("combine", 3),
)
EARLY = (0, 1)
MESH = pl.DeviceIdType.MESH
F32 = jnp.float32
BF16 = jnp.bfloat16


def iota(shape, axis):
    return lax.broadcasted_iota(jnp.int32, shape, axis)


def kernel(
    q_ref, res_ref, kv_hbm, len_ref, ids_ref, rw_ref, gain_ref, wgu_hbm, wd_hbm,
    out_ref,
    qf, sc, att, hid, ns, tmp_i, tmp_w, sel, wt_hi, wt_lo, acc,
    disp, arr, rsend, ret, x, pf, sa, ta, sb, fin,
    wraw, wgu, wd, kv_ref,
    kv_sem, w_sem, p_send, p_recv, d_send, d_recv, g_send, g_recv, r_send, r_recv, e_send, e_recv,
):
    side = lax.axis_index("side")
    col = lax.axis_index("col")
    hidx = lax.axis_index("hid")
    zc = col // NY
    yc = lax.rem(col, NY)
    rows, width = res_ref.shape
    half = width // 2

    def column(i, sign):
        dz, dy = DZ[i // NY], i % NY
        return lax.rem(zc + (sign * dz + NZ), NZ) * NY + lax.rem(yc + (sign * dy + NY), NY)

    def on_col(i, sign):
        return {"side": side, "col": column(i, sign), "hid": hidx}

    up = {"side": side, "col": col, "hid": lax.rem(hidx + 1, NX)}
    down = {"side": side, "col": col, "hid": lax.rem(hidx + NX - 1, NX)}
    partner = {"side": 1 - side, "col": col, "hid": hidx}

    def remote(src, dst, send, recv, device):
        return pltpu.make_async_remote_copy(
            src_ref=src, dst_ref=dst, send_sem=send, recv_sem=recv,
            device_id=device, device_id_type=MESH,
        )

    begun, landed = [], set()

    def start(make, *key):
        make(*key).start()
        begun.append((make, key))

    def arrive(make, *key):
        make(*key).wait_recv()
        landed.add((make, key))

    kv_copy = pltpu.make_async_copy(kv_hbm, kv_ref, kv_sem)
    kv_copy.start()

    barrier = pltpu.get_barrier_semaphore()
    for device in [on_col(i, 1) for i in range(1, COLS)] + [up, down, partner]:
        pl.semaphore_signal(barrier, inc=1, device_id=device, device_id_type=MESH)

    w_copies = [
        pltpu.make_async_copy(
            wgu_hbm.at[:, :, pl.ds(l * 128, 128)],
            wraw.at[l],
            w_sem.at[l],
        )
        for l in range(3)
    ] + [pltpu.make_async_copy(wd_hbm, wd.at[pl.ds(0, 384)], w_sem.at[3])]
    for copy in w_copies:
        copy.start()

    tmp_i[...] = jnp.zeros_like(tmp_i)
    tmp_w[...] = jnp.zeros_like(tmp_w)
    tmp_i[0:3, 0:rows] = ids_ref[...]
    tmp_w[0:3, 0:rows] = rw_ref[...]
    ids_all = tmp_i[...]
    w_all = tmp_w[...]
    for shift in (16, 32, 64):
        ids_all = ids_all + pltpu.roll(ids_all, shift, 1)
        w_all = w_all + pltpu.roll(w_all, shift, 1)
    square = (128, 128)
    lane, sub = iota(square, 1), iota(square, 0)
    earlier = jnp.where(
        ((sub >> 4) == (lane >> 4)) & ((sub & 15) < (lane & 15)), 1.0, 0.0
    ).astype(BF16)
    same_part = (sub & 7) == (lane >> 4)
    rank_want = ((sub >> 3) & 1).astype(F32)
    def expert_of(g):
        dz = jnp.where((sub >> 6) == 0, DZ[2 * g], DZ[2 * g + 1])
        dy = (sub >> 4) & 3
        return ((zc + dz + NZ) & (NZ - 1)) * NY + ((yc + dy) & (NY - 1))

    for g in range(GROUPS):
        expert = expert_of(g)
        named = jnp.zeros(square, F32)
        for k in range(3):
            named = named + jnp.where(expert == ids_all[k : k + 1, :], 1.0, 0.0)
        rank = jnp.dot(named.astype(BF16), earlier, preferred_element_type=F32)
        here = (named > 0.5) & (jnp.abs(rank - rank_want) < 0.5) & same_part
        sel[g] = jnp.where(here, 1.0, 0.0).astype(BF16)

    def weigh(g):
        expert = expert_of(g)
        weight = jnp.zeros(square, F32)
        for k in range(3):
            weight = weight + jnp.where(expert == ids_all[k : k + 1, :], w_all[k : k + 1, :], 0.0)
        weight_t = (weight * sel[g].astype(F32)).T
        top_part = weight_t.astype(BF16)
        wt_hi[g] = top_part
        wt_lo[g] = (weight_t - top_part.astype(F32)).astype(BF16)

    for head in range(HEADS):
        qf[pl.ds(head * rows, rows), :] = q_ref[:, pl.ds(head * HD, HD)].astype(F32)
    kv_copy.wait()
    positions = iota((HEADS, kv_ref.shape[1]), 1)
    for r in range(rows):
        q_r = qf[pl.ds(r, HEADS, stride=rows), :].astype(BF16)
        s_r = lax.dot_general(
            q_r, kv_ref[r, :, 0:HD], (((1,), (1,)), ((), ())), preferred_element_type=F32
        ) * (1.0 / math.sqrt(HD))
        sc[pl.ds(r * HEADS, HEADS), :] = jnp.where(positions < len_ref[r], s_r, -1e30)
    for r in range(rows):
        s_r = sc[pl.ds(r * HEADS, HEADS), :]
        e_r = jnp.exp(s_r - jnp.max(s_r, axis=1, keepdims=True))
        p_r = (e_r / jnp.sum(e_r, axis=1, keepdims=True)).astype(BF16)
        att[pl.ds(r, HEADS, stride=rows), :] = jnp.dot(
            p_r, kv_ref[r, :, HD : 2 * HD], preferred_element_type=F32
        )
    total = jnp.zeros((rows, HD), F32)
    for head in range(HEADS):
        lanes = pl.ds(head * HD, HD)
        h_part = res_ref[:, lanes].astype(F32) + att[pl.ds(head * rows, rows), :]
        hid[:, lanes] = h_part
        total = total + h_part * h_part
    scale = lax.rsqrt(jnp.sum(total, axis=1, keepdims=True) * (1.0 / width) + 1e-6)
    for j in range(PER):
        lanes = pl.ds(j * CHUNK, CHUNK)
        ns[pl.ds(j * rows, rows), :] = (hid[:, lanes] * scale * gain_ref[:, lanes]).astype(BF16)

    def d_copy(i):
        return remote(disp.at[i], arr.at[i], d_send.at[i], d_recv.at[i], on_col(i, 1))

    def send(g):
        for i in range(max(1, g * PER), (g + 1) * PER):
            start(d_copy, i)

    pl.semaphore_wait(barrier, COLS - 1 + 3)
    for g in range(GROUPS):
        block = jnp.dot(sel[g], ns[...], preferred_element_type=F32).astype(BF16)
        for k in range(PER):
            i = g * PER + k
            piece = block[k * 16 : (k + 1) * 16, :]
            if i == 0:
                arr[0] = piece
            else:
                disp[i] = piece
        if g in EARLY:
            send(g)

    to_rows = jnp.where(
        lane == ((sub & 15) >> 1) * 16 + (sub & 1) * 8 + (sub >> 4), 1.0, 0.0
    ).astype(BF16)
    to_blocks = jnp.where(
        lane == (sub & 7) * 16 + (sub >> 4) * 2 + ((sub >> 3) & 1), 1.0, 0.0
    ).astype(BF16)

    wide = (256, 256)
    apart = jnp.where(
        iota(wide, 1) == 2 * (iota(wide, 0) & 127) + (iota(wide, 0) >> 7), 1.0, 0.0
    ).astype(BF16)

    def p_copy(which):
        if which == 4:
            src, dst = wd.at[pl.ds(0, 384)], wd.at[pl.ds(384, 384)]
        else:
            deep = pl.ds(which * 1024, 1024)
            src, dst = wgu.at[0, :, deep, :], wgu.at[1, :, deep, :]
        return remote(src, dst, p_send.at[which], p_recv.at[which], partner)

    def take_apart(part):
        if part == 0:
            w_copies[3].wait()
            start(p_copy, 4)
            for l in range(3):
                w_copies[l].wait()
        raws = [wraw.at[l].reshape(8192, 128) for l in range(3)]

        def body(t, carry):
            first = part * 2048 + t * 512
            both = jnp.concatenate(
                [raw[pl.ds(pl.multiple_of(first + d, 256), 256), :] for d in (0, 256) for raw in raws],
                axis=1,
            )
            pair = jnp.dot(apart, both, preferred_element_type=F32).astype(BF16)
            for d in range(2):
                there = pl.ds(pl.multiple_of(part * 1024 + t * 256 + d * 128, 128), 128)
                for l in range(3):
                    lanes = slice((d * 3 + l) * 128, (d * 3 + l + 1) * 128)
                    wgu[0, l, there, 0:128] = pair[0:128, lanes]
                    wgu[0, l, there, 128:256] = pair[128:256, lanes]
            return carry

        lax.fori_loop(0, 4, body, 0, unroll=2)
        start(p_copy, part)

    low, high = pl.ds(0, half), pl.ds(half, half)

    def g_copy(g, which):
        src, dst, device = {
            0: (x.at[g, 0, :, low], x.at[g, 1, :, low], up),
            1: (x.at[g, 0, :, high], x.at[g, 1, :, high], up),
            2: (x.at[g, 0, :, high], x.at[g, 2, :, high], down),
            3: (x.at[g, 0, :, low], x.at[g, 2, :, low], down),
            4: (x.at[g, 1, :, low], x.at[g, 3, :, low], up),
            5: (x.at[g, 2, :, high], x.at[g, 3, :, high], down),
        }[which]
        return remote(src, dst, g_send.at[g, which], g_recv.at[g, which], device)

    def gather_own(g):
        for i in range(max(1, g * PER), (g + 1) * PER):
            arrive(d_copy, i)
        blocks = arr[pl.ds(g * PER, PER)].reshape(128, CHUNK)
        rows_g = jnp.dot(to_rows, blocks, preferred_element_type=F32).astype(BF16)
        for j in range(PER):
            x[g, 0, :, pl.ds(j * CHUNK, CHUNK)] = rows_g[j * 16 : (j + 1) * 16, :]
        for which in (0, 2, 1, 3):
            start(g_copy, g, which)

    def on_up(g):
        arrive(g_copy, g, 0)
        start(g_copy, g, 4)

    def on_down(g):
        arrive(g_copy, g, 2)
        start(g_copy, g, 5)

    def r_copy(g, which):
        src, dst, device = {
            0: (sa.at[g, 0], ta.at[g, 0], up),
            1: (sa.at[g, 1], ta.at[g, 1], down),
            2: (sa.at[g, 2], fin.at[g, 0, :, high], up),
            3: (sa.at[g, 3], fin.at[g, 1, :, low], down),
            4: (sb.at[g, 0], fin.at[g, 0, :, low], up),
            5: (sb.at[g, 1], fin.at[g, 1, :, high], down),
        }[which]
        return remote(src, dst, r_send.at[g, which], r_recv.at[g, which], device)

    def experts(g):
        if not ready:
            for which in range(5):
                arrive(p_copy, which)
            ready.append(True)
        for which in (1, 3, 4, 5):
            arrive(g_copy, g, which)
        rows_g = x[g].reshape(64, width)
        parts = []
        for core in range(2):
            for l in range(3):
                both = jnp.dot(rows_g, wgu[core, l], preferred_element_type=F32)
                gate, upper = both[:, 0:128], both[:, 128:256]
                parts.append((gate / (1.0 + jnp.exp(-gate)) * upper).astype(BF16))
        act = jnp.concatenate(parts, axis=1)
        for n in range(8):
            lanes = pl.ds(n * CHUNK, CHUNK)
            there = pl.ds(n % 4 * CHUNK, CHUNK)
            part = jnp.dot(act, wd[:, lanes], preferred_element_type=F32)
            pf[g, 0:16, lanes] = part[0:16, :]
            if n < 4:
                sa[g, 0, :, there] = part[48:64, :].astype(BF16)
                sa[g, 3, :, there] = part[16:32, :].astype(BF16)
                pf[g, 32:48, lanes] = part[32:48, :]
            else:
                sa[g, 1, :, there] = part[48:64, :].astype(BF16)
                sa[g, 2, :, there] = part[32:48, :].astype(BF16)
                pf[g, 16:32, lanes] = part[16:32, :]
            if n == 3:
                start(r_copy, g, 0)
                start(r_copy, g, 3)
        start(r_copy, g, 1)
        start(r_copy, g, 2)

    def pass_up(g):
        arrive(r_copy, g, 0)
        sb[g, 0] = (pf[g, 32:48, low] + ta[g, 0].astype(F32)).astype(BF16)
        start(r_copy, g, 4)

    def pass_down(g):
        arrive(r_copy, g, 1)
        sb[g, 1] = (pf[g, 16:32, high] + ta[g, 1].astype(F32)).astype(BF16)
        start(r_copy, g, 5)

    def e_copy(i):
        return remote(rsend.at[i], ret.at[i], e_send.at[i], e_recv.at[i], on_col(i, -1))

    def give_back(g):
        for which in (2, 3, 4, 5):
            arrive(r_copy, g, which)
        pieces = []
        for j in range(PER):
            lanes = pl.ds(j * CHUNK, CHUNK)
            whole = pf[g, 0:16, lanes] + fin[g, 0, :, lanes].astype(F32) + fin[g, 1, :, lanes].astype(F32)
            pieces.append(whole.astype(BF16))
        blocks = jnp.dot(
            to_blocks, jnp.concatenate(pieces, axis=0), preferred_element_type=F32
        ).astype(BF16)
        for k in range(PER):
            i = g * PER + k
            piece = blocks[k * 16 : (k + 1) * 16, :]
            if i == 0:
                ret[0] = piece
            else:
                rsend[i] = piece
        for i in range(max(1, g * PER), (g + 1) * PER):
            start(e_copy, i)

    def combine(g):
        for i in range(max(1, g * PER), (g + 1) * PER):
            arrive(e_copy, i)
        blocks = ret[pl.ds(g * PER, PER)].reshape(128, CHUNK)
        part = jnp.dot(wt_hi[g], blocks, preferred_element_type=F32) + jnp.dot(
            wt_lo[g], blocks, preferred_element_type=F32
        )
        if not summed:
            summed.append(True)
            acc[...] = part
        else:
            acc[...] = acc[...] + part

    steps = {
        "send": send, "weigh": weigh, "apart": take_apart, "own": gather_own, "up": on_up, "down": on_down,
        "experts": experts, "pass_up": pass_up, "pass_down": pass_down, "back": give_back,
        "combine": combine,
    }
    ready, summed = [], []
    for name, number in SCHEDULE:
        steps[name](number)

    for j in range(PER):
        lanes = pl.ds(j * CHUNK, CHUNK)
        out_ref[:, lanes] = (hid[:, lanes] + acc[pl.ds(j * rows, rows), :]).astype(BF16)

    for make, key in begun:
        make(*key).wait_send()


def on_device(
    residual, queries, key_values, lengths, route_ids, route_weights, norm_gain, w_gate_up, w_down
):
    rows, width = residual.shape
    vmem = pl.BlockSpec(memory_space=pltpu.VMEM)
    anywhere = pl.BlockSpec(memory_space=pl.ANY)
    half = width // 2
    return pl.pallas_call(
        kernel,
        out_shape=jax.ShapeDtypeStruct((rows, width), BF16),
        in_specs=[
            vmem, vmem, anywhere, pl.BlockSpec(memory_space=pltpu.SMEM), vmem, vmem, vmem,
            anywhere, anywhere,
        ],
        out_specs=vmem,
        scratch_shapes=[
            pltpu.VMEM((HEADS * rows, HD), F32),
            pltpu.VMEM((HEADS * rows, key_values.shape[1]), F32),
            pltpu.VMEM((HEADS * rows, HD), F32),
            pltpu.VMEM((rows, width), F32),
            pltpu.VMEM((PER * rows, CHUNK), BF16),
            pltpu.VMEM((8, 128), jnp.int32),
            pltpu.VMEM((8, 128), F32),
            pltpu.VMEM((GROUPS, 128, 128), BF16),
            pltpu.VMEM((GROUPS, 128, 128), BF16),
            pltpu.VMEM((GROUPS, 128, 128), BF16),
            pltpu.VMEM((PER * rows, CHUNK), F32),
            pltpu.VMEM((COLS, 16, CHUNK), BF16),
            pltpu.VMEM((COLS, 16, CHUNK), BF16),
            pltpu.VMEM((COLS, 16, CHUNK), BF16),
            pltpu.VMEM((COLS, 16, CHUNK), BF16),
            pltpu.VMEM((GROUPS, 4, 16, width), BF16),
            pltpu.VMEM((GROUPS, 48, width), F32),
            pltpu.VMEM((GROUPS, 4, 16, half), BF16),
            pltpu.VMEM((GROUPS, 2, 16, half), BF16),
            pltpu.VMEM((GROUPS, 2, 16, half), BF16),
            pltpu.VMEM((GROUPS, 2, 16, width), BF16),
            pltpu.VMEM((3, 4096, 2, 128), BF16),
            pltpu.VMEM((2, 3, 4096, 256), BF16),
            pltpu.VMEM((768, 4096), BF16),
            pltpu.VMEM(key_values.shape, BF16),
            pltpu.SemaphoreType.DMA,
            pltpu.SemaphoreType.DMA((4,)),
            pltpu.SemaphoreType.DMA((5,)),
            pltpu.SemaphoreType.DMA((5,)),
            pltpu.SemaphoreType.DMA((COLS,)),
            pltpu.SemaphoreType.DMA((COLS,)),
            pltpu.SemaphoreType.DMA((GROUPS, 6)),
            pltpu.SemaphoreType.DMA((GROUPS, 6)),
            pltpu.SemaphoreType.DMA((GROUPS, 6)),
            pltpu.SemaphoreType.DMA((GROUPS, 6)),
            pltpu.SemaphoreType.DMA((COLS,)),
            pltpu.SemaphoreType.DMA((COLS,)),
        ],
        compiler_params=pltpu.CompilerParams(
            collective_id=0, has_side_effects=True, vmem_limit_bytes=60 * 2**20
        ),
        name="moe_step",
    )(
        queries, residual, key_values, lengths, route_ids.T, route_weights.T,
        norm_gain.reshape(1, width), w_gate_up[0], w_down[0],
    )


def solution(mesh):
    placed = (
        P(("side", "col", "hid"), None),
        P(("side", "col", "hid"), None),
        P(("side", "col", "hid"), None, None),
        P(("side", "col", "hid")),
        P(("side", "col", "hid"), None),
        P(("side", "col", "hid"), None),
        P(),
        P("col", None, None, ("side", "hid")),
        P("col", ("side", "hid"), None),
    )
    return jax.shard_map(
        on_device,
        mesh=mesh,
        in_specs=placed,
        out_specs=P(("side", "col", "hid"), None),
        check_vma=False,
    )
```

```python
import math

import jax
import jax.numpy as jnp
from jax import lax
from jax.experimental import pallas as pl
from jax.experimental.pallas import tpu as pltpu
from jax.sharding import PartitionSpec as P

HEADS = 32
HD = 128
COLS = 32
NY = 4
NZ = 8
NX = 4
GROUPS = 4
PER = 8
CHUNK = 512
DZ = (0, 1, -2, 3, -3, 4, -1, 2)
SCHEDULE = (
    ("apart", 0), ("send", 2), ("apart", 1), ("send", 3), ("own", 0),
    ("apart", 2), ("apart", 3), ("down", 0), ("up", 0), ("weigh", 0),
    ("weigh", 1), ("weigh", 2), ("weigh", 3), ("own", 1), ("own", 2),
    ("up", 1), ("down", 1), ("own", 3), ("up", 2), ("down", 2),
    ("experts", 1), ("down", 3), ("up", 3), ("experts", 2), ("pass_down", 1),
    ("pass_up", 1), ("experts", 0), ("pass_up", 2), ("pass_down", 2), ("back", 1),
    ("experts", 3), ("back", 2), ("pass_up", 0), ("pass_down", 0), ("pass_up", 3),
    ("pass_down", 3), ("back", 0), ("back", 3), ("combine", 0), ("combine", 1),
    ("combine", 2), ("combine", 3),
)
EARLY = (0, 1)
MESH = pl.DeviceIdType.MESH
F32 = jnp.float32
BF16 = jnp.bfloat16


def iota(shape, axis):
    return lax.broadcasted_iota(jnp.int32, shape, axis)


def kernel(
    q_ref, res_ref, kv_hbm, len_ref, ids_ref, rw_ref, gain_ref, wgu_hbm, wd_hbm,
    out_ref,
    qf, sc, att, hid, ns, tmp_i, tmp_w, sel, wt_hi, wt_lo, acc,
    disp, arr, rsend, ret, x, pf, sa, ta, sb, fin,
    wraw, wgu, wd, kv_ref,
    kv_sem, w_sem, p_send, p_recv, d_send, d_recv, g_send, g_recv, r_send, r_recv, e_send, e_recv,
):
    side = lax.axis_index("side")
    col = lax.axis_index("col")
    hidx = lax.axis_index("hid")
    zc = col // NY
    yc = lax.rem(col, NY)
    rows, width = res_ref.shape
    half = width // 2

    def column(i, sign):
        dz, dy = DZ[i // NY], i % NY
        return lax.rem(zc + (sign * dz + NZ), NZ) * NY + lax.rem(yc + (sign * dy + NY), NY)

    def on_col(i, sign):
        return {"side": side, "col": column(i, sign), "hid": hidx}

    up = {"side": side, "col": col, "hid": lax.rem(hidx + 1, NX)}
    down = {"side": side, "col": col, "hid": lax.rem(hidx + NX - 1, NX)}
    partner = {"side": 1 - side, "col": col, "hid": hidx}

    def remote(src, dst, send, recv, device):
        return pltpu.make_async_remote_copy(
            src_ref=src, dst_ref=dst, send_sem=send, recv_sem=recv,
            device_id=device, device_id_type=MESH,
        )

    begun, landed = [], set()

    def start(make, *key):
        make(*key).start()
        begun.append((make, key))

    def arrive(make, *key):
        make(*key).wait_recv()
        landed.add((make, key))

    kv_copy = pltpu.make_async_copy(kv_hbm, kv_ref, kv_sem)
    kv_copy.start()

    barrier = pltpu.get_barrier_semaphore()
    for device in [on_col(i, 1) for i in range(1, COLS)] + [up, down, partner]:
        pl.semaphore_signal(barrier, inc=1, device_id=device, device_id_type=MESH)

    w_copies = [
        pltpu.make_async_copy(
            wgu_hbm.at[:, :, pl.ds(l * 128, 128)],
            wraw.at[l],
            w_sem.at[l],
        )
        for l in range(3)
    ] + [pltpu.make_async_copy(wd_hbm, wd.at[pl.ds(0, 384)], w_sem.at[3])]
    for copy in w_copies:
        copy.start()

    tmp_i[...] = jnp.zeros_like(tmp_i)
    tmp_w[...] = jnp.zeros_like(tmp_w)
    tmp_i[0:3, 0:rows] = ids_ref[...]
    tmp_w[0:3, 0:rows] = rw_ref[...]
    ids_all = tmp_i[...]
    w_all = tmp_w[...]
    for shift in (16, 32, 64):
        ids_all = ids_all + pltpu.roll(ids_all, shift, 1)
        w_all = w_all + pltpu.roll(w_all, shift, 1)
    square = (128, 128)
    lane, sub = iota(square, 1), iota(square, 0)
    earlier = jnp.where(
        ((sub >> 4) == (lane >> 4)) & ((sub & 15) < (lane & 15)), 1.0, 0.0
    ).astype(BF16)
    same_part = (sub & 7) == (lane >> 4)
    rank_want = ((sub >> 3) & 1).astype(F32)
    def expert_of(g):
        dz = jnp.where((sub >> 6) == 0, DZ[2 * g], DZ[2 * g + 1])
        dy = (sub >> 4) & 3
        return ((zc + dz + NZ) & (NZ - 1)) * NY + ((yc + dy) & (NY - 1))

    for g in range(GROUPS):
        expert = expert_of(g)
        named = jnp.zeros(square, F32)
        for k in range(3):
            named = named + jnp.where(expert == ids_all[k : k + 1, :], 1.0, 0.0)
        rank = jnp.dot(named.astype(BF16), earlier, preferred_element_type=F32)
        here = (named > 0.5) & (jnp.abs(rank - rank_want) < 0.5) & same_part
        sel[g] = jnp.where(here, 1.0, 0.0).astype(BF16)

    def weigh(g):
        expert = expert_of(g)
        weight = jnp.zeros(square, F32)
        for k in range(3):
            weight = weight + jnp.where(expert == ids_all[k : k + 1, :], w_all[k : k + 1, :], 0.0)
        weight_t = (weight * sel[g].astype(F32)).T
        top_part = weight_t.astype(BF16)
        wt_hi[g] = top_part
        wt_lo[g] = (weight_t - top_part.astype(F32)).astype(BF16)

    for head in range(HEADS):
        qf[pl.ds(head * rows, rows), :] = q_ref[:, pl.ds(head * HD, HD)].astype(F32)
    kv_copy.wait()
    positions = iota((HEADS, kv_ref.shape[1]), 1)
    for r in range(rows):
        q_r = qf[pl.ds(r, HEADS, stride=rows), :].astype(BF16)
        s_r = lax.dot_general(
            q_r, kv_ref[r, :, 0:HD], (((1,), (1,)), ((), ())), preferred_element_type=F32
        ) * (1.0 / math.sqrt(HD))
        sc[pl.ds(r * HEADS, HEADS), :] = jnp.where(positions < len_ref[r], s_r, -1e30)
    for r in range(rows):
        s_r = sc[pl.ds(r * HEADS, HEADS), :]
        e_r = jnp.exp(s_r - jnp.max(s_r, axis=1, keepdims=True))
        p_r = (e_r / jnp.sum(e_r, axis=1, keepdims=True)).astype(BF16)
        att[pl.ds(r, HEADS, stride=rows), :] = jnp.dot(
            p_r, kv_ref[r, :, HD : 2 * HD], preferred_element_type=F32
        )
    total = jnp.zeros((rows, HD), F32)
    for head in range(HEADS):
        lanes = pl.ds(head * HD, HD)
        h_part = res_ref[:, lanes].astype(F32) + att[pl.ds(head * rows, rows), :]
        hid[:, lanes] = h_part
        total = total + h_part * h_part
    scale = lax.rsqrt(jnp.sum(total, axis=1, keepdims=True) * (1.0 / width) + 1e-6)
    for j in range(PER):
        lanes = pl.ds(j * CHUNK, CHUNK)
        ns[pl.ds(j * rows, rows), :] = (hid[:, lanes] * scale * gain_ref[:, lanes]).astype(BF16)

    def d_copy(i):
        return remote(disp.at[i], arr.at[i], d_send.at[i], d_recv.at[i], on_col(i, 1))

    def send(g):
        for i in reversed(range(max(1, g * PER), (g + 1) * PER)):
            start(d_copy, i)

    pl.semaphore_wait(barrier, COLS - 1 + 3)
    for g in range(GROUPS):
        block = jnp.dot(sel[g], ns[...], preferred_element_type=F32).astype(BF16)
        for k in range(PER):
            i = g * PER + k
            piece = block[k * 16 : (k + 1) * 16, :]
            if i == 0:
                arr[0] = piece
            else:
                disp[i] = piece
        if g in EARLY:
            send(g)

    to_rows = jnp.where(
        lane == ((sub & 15) >> 1) * 16 + (sub & 1) * 8 + (sub >> 4), 1.0, 0.0
    ).astype(BF16)
    to_blocks = jnp.where(
        lane == (sub & 7) * 16 + (sub >> 4) * 2 + ((sub >> 3) & 1), 1.0, 0.0
    ).astype(BF16)

    wide = (256, 256)
    apart = jnp.where(
        iota(wide, 1) == 2 * (iota(wide, 0) & 127) + (iota(wide, 0) >> 7), 1.0, 0.0
    ).astype(BF16)

    def p_copy(which):
        if which == 4:
            src, dst = wd.at[pl.ds(0, 384)], wd.at[pl.ds(384, 384)]
        else:
            deep = pl.ds(which * 1024, 1024)
            src, dst = wgu.at[0, :, deep, :], wgu.at[1, :, deep, :]
        return remote(src, dst, p_send.at[which], p_recv.at[which], partner)

    def take_apart(part):
        if part == 0:
            w_copies[3].wait()
            start(p_copy, 4)
            for l in range(3):
                w_copies[l].wait()
        raws = [wraw.at[l].reshape(8192, 128) for l in range(3)]

        def body(t, carry):
            first = part * 2048 + t * 512
            both = jnp.concatenate(
                [raw[pl.ds(pl.multiple_of(first + d, 256), 256), :] for d in (0, 256) for raw in raws],
                axis=1,
            )
            pair = jnp.dot(apart, both, preferred_element_type=F32).astype(BF16)
            for d in range(2):
                there = pl.ds(pl.multiple_of(part * 1024 + t * 256 + d * 128, 128), 128)
                for l in range(3):
                    lanes = slice((d * 3 + l) * 128, (d * 3 + l + 1) * 128)
                    wgu[0, l, there, 0:128] = pair[0:128, lanes]
                    wgu[0, l, there, 128:256] = pair[128:256, lanes]
            return carry

        lax.fori_loop(0, 4, body, 0, unroll=2)
        start(p_copy, part)

    low, high = pl.ds(0, half), pl.ds(half, half)

    def g_copy(g, which):
        src, dst, device = {
            0: (x.at[g, 0, :, low], x.at[g, 1, :, low], up),
            1: (x.at[g, 0, :, high], x.at[g, 1, :, high], up),
            2: (x.at[g, 0, :, high], x.at[g, 2, :, high], down),
            3: (x.at[g, 0, :, low], x.at[g, 2, :, low], down),
            4: (x.at[g, 1, :, low], x.at[g, 3, :, low], up),
            5: (x.at[g, 2, :, high], x.at[g, 3, :, high], down),
        }[which]
        return remote(src, dst, g_send.at[g, which], g_recv.at[g, which], device)

    def gather_own(g):
        for i in range(max(1, g * PER), (g + 1) * PER):
            arrive(d_copy, i)
        blocks = arr[pl.ds(g * PER, PER)].reshape(128, CHUNK)
        rows_g = jnp.dot(to_rows, blocks, preferred_element_type=F32).astype(BF16)
        for j in range(PER):
            x[g, 0, :, pl.ds(j * CHUNK, CHUNK)] = rows_g[j * 16 : (j + 1) * 16, :]
        for which in (0, 2, 1, 3):
            start(g_copy, g, which)

    def on_up(g):
        arrive(g_copy, g, 0)
        start(g_copy, g, 4)

    def on_down(g):
        arrive(g_copy, g, 2)
        start(g_copy, g, 5)

    def r_copy(g, which):
        src, dst, device = {
            0: (sa.at[g, 0], ta.at[g, 0], up),
            1: (sa.at[g, 1], ta.at[g, 1], down),
            2: (sa.at[g, 2], fin.at[g, 0, :, high], up),
            3: (sa.at[g, 3], fin.at[g, 1, :, low], down),
            4: (sb.at[g, 0], fin.at[g, 0, :, low], up),
            5: (sb.at[g, 1], fin.at[g, 1, :, high], down),
        }[which]
        return remote(src, dst, r_send.at[g, which], r_recv.at[g, which], device)

    def experts(g):
        if not ready:
            for which in range(5):
                arrive(p_copy, which)
            ready.append(True)
        for which in (1, 3, 4, 5):
            arrive(g_copy, g, which)
        rows_g = x[g].reshape(64, width)
        parts = []
        for core in range(2):
            for l in range(3):
                both = jnp.dot(rows_g, wgu[core, l], preferred_element_type=F32)
                gate, upper = both[:, 0:128], both[:, 128:256]
                parts.append((gate / (1.0 + jnp.exp(-gate)) * upper).astype(BF16))
        act = jnp.concatenate(parts, axis=1)
        for n in range(8):
            lanes = pl.ds(n * CHUNK, CHUNK)
            there = pl.ds(n % 4 * CHUNK, CHUNK)
            part = jnp.dot(act, wd[:, lanes], preferred_element_type=F32)
            pf[g, 0:16, lanes] = part[0:16, :]
            if n < 4:
                sa[g, 0, :, there] = part[48:64, :].astype(BF16)
                sa[g, 3, :, there] = part[16:32, :].astype(BF16)
                pf[g, 32:48, lanes] = part[32:48, :]
            else:
                sa[g, 1, :, there] = part[48:64, :].astype(BF16)
                sa[g, 2, :, there] = part[32:48, :].astype(BF16)
                pf[g, 16:32, lanes] = part[16:32, :]
            if n == 3:
                start(r_copy, g, 0)
                start(r_copy, g, 3)
        start(r_copy, g, 1)
        start(r_copy, g, 2)

    def pass_up(g):
        arrive(r_copy, g, 0)
        sb[g, 0] = (pf[g, 32:48, low] + ta[g, 0].astype(F32)).astype(BF16)
        start(r_copy, g, 4)

    def pass_down(g):
        arrive(r_copy, g, 1)
        sb[g, 1] = (pf[g, 16:32, high] + ta[g, 1].astype(F32)).astype(BF16)
        start(r_copy, g, 5)

    def e_copy(i):
        return remote(rsend.at[i], ret.at[i], e_send.at[i], e_recv.at[i], on_col(i, -1))

    def give_back(g):
        for which in (2, 3, 4, 5):
            arrive(r_copy, g, which)
        pieces = []
        for j in range(PER):
            lanes = pl.ds(j * CHUNK, CHUNK)
            whole = pf[g, 0:16, lanes] + fin[g, 0, :, lanes].astype(F32) + fin[g, 1, :, lanes].astype(F32)
            pieces.append(whole.astype(BF16))
        blocks = jnp.dot(
            to_blocks, jnp.concatenate(pieces, axis=0), preferred_element_type=F32
        ).astype(BF16)
        for k in range(PER):
            i = g * PER + k
            piece = blocks[k * 16 : (k + 1) * 16, :]
            if i == 0:
                ret[0] = piece
            else:
                rsend[i] = piece
        for i in reversed(range(max(1, g * PER), (g + 1) * PER)):
            start(e_copy, i)

    def combine(g):
        for i in range(max(1, g * PER), (g + 1) * PER):
            arrive(e_copy, i)
        blocks = ret[pl.ds(g * PER, PER)].reshape(128, CHUNK)
        part = jnp.dot(wt_hi[g], blocks, preferred_element_type=F32) + jnp.dot(
            wt_lo[g], blocks, preferred_element_type=F32
        )
        if not summed:
            summed.append(True)
            acc[...] = part
        else:
            acc[...] = acc[...] + part

    steps = {
        "send": send, "weigh": weigh, "apart": take_apart, "own": gather_own, "up": on_up, "down": on_down,
        "experts": experts, "pass_up": pass_up, "pass_down": pass_down, "back": give_back,
        "combine": combine,
    }
    ready, summed = [], []
    for name, number in SCHEDULE:
        steps[name](number)

    for j in range(PER):
        lanes = pl.ds(j * CHUNK, CHUNK)
        out_ref[:, lanes] = (hid[:, lanes] + acc[pl.ds(j * rows, rows), :]).astype(BF16)

    for make, key in begun:
        make(*key).wait_send()


def on_device(
    residual, queries, key_values, lengths, route_ids, route_weights, norm_gain, w_gate_up, w_down
):
    rows, width = residual.shape
    vmem = pl.BlockSpec(memory_space=pltpu.VMEM)
    anywhere = pl.BlockSpec(memory_space=pl.ANY)
    half = width // 2
    return pl.pallas_call(
        kernel,
        out_shape=jax.ShapeDtypeStruct((rows, width), BF16),
        in_specs=[
            vmem, vmem, anywhere, pl.BlockSpec(memory_space=pltpu.SMEM), vmem, vmem, vmem,
            anywhere, anywhere,
        ],
        out_specs=vmem,
        scratch_shapes=[
            pltpu.VMEM((HEADS * rows, HD), F32),
            pltpu.VMEM((HEADS * rows, key_values.shape[1]), F32),
            pltpu.VMEM((HEADS * rows, HD), F32),
            pltpu.VMEM((rows, width), F32),
            pltpu.VMEM((PER * rows, CHUNK), BF16),
            pltpu.VMEM((8, 128), jnp.int32),
            pltpu.VMEM((8, 128), F32),
            pltpu.VMEM((GROUPS, 128, 128), BF16),
            pltpu.VMEM((GROUPS, 128, 128), BF16),
            pltpu.VMEM((GROUPS, 128, 128), BF16),
            pltpu.VMEM((PER * rows, CHUNK), F32),
            pltpu.VMEM((COLS, 16, CHUNK), BF16),
            pltpu.VMEM((COLS, 16, CHUNK), BF16),
            pltpu.VMEM((COLS, 16, CHUNK), BF16),
            pltpu.VMEM((COLS, 16, CHUNK), BF16),
            pltpu.VMEM((GROUPS, 4, 16, width), BF16),
            pltpu.VMEM((GROUPS, 48, width), F32),
            pltpu.VMEM((GROUPS, 4, 16, half), BF16),
            pltpu.VMEM((GROUPS, 2, 16, half), BF16),
            pltpu.VMEM((GROUPS, 2, 16, half), BF16),
            pltpu.VMEM((GROUPS, 2, 16, width), BF16),
            pltpu.VMEM((3, 4096, 2, 128), BF16),
            pltpu.VMEM((2, 3, 4096, 256), BF16),
            pltpu.VMEM((768, 4096), BF16),
            pltpu.VMEM(key_values.shape, BF16),
            pltpu.SemaphoreType.DMA,
            pltpu.SemaphoreType.DMA((4,)),
            pltpu.SemaphoreType.DMA((5,)),
            pltpu.SemaphoreType.DMA((5,)),
            pltpu.SemaphoreType.DMA((COLS,)),
            pltpu.SemaphoreType.DMA((COLS,)),
            pltpu.SemaphoreType.DMA((GROUPS, 6)),
            pltpu.SemaphoreType.DMA((GROUPS, 6)),
            pltpu.SemaphoreType.DMA((GROUPS, 6)),
            pltpu.SemaphoreType.DMA((GROUPS, 6)),
            pltpu.SemaphoreType.DMA((COLS,)),
            pltpu.SemaphoreType.DMA((COLS,)),
        ],
        compiler_params=pltpu.CompilerParams(
            collective_id=0, has_side_effects=True, vmem_limit_bytes=60 * 2**20
        ),
        name="moe_step",
    )(
        queries, residual, key_values, lengths, route_ids.T, route_weights.T,
        norm_gain.reshape(1, width), w_gate_up[0], w_down[0],
    )


def solution(mesh):
    placed = (
        P(("side", "col", "hid"), None),
        P(("side", "col", "hid"), None),
        P(("side", "col", "hid"), None, None),
        P(("side", "col", "hid")),
        P(("side", "col", "hid"), None),
        P(("side", "col", "hid"), None),
        P(),
        P("col", None, None, ("side", "hid")),
        P("col", ("side", "hid"), None),
    )
    return jax.shard_map(
        on_device,
        mesh=mesh,
        in_specs=placed,
        out_specs=P(("side", "col", "hid"), None),
        check_vma=False,
    )
```
